512 devices in a mesh: seq: 64 (over y_lo, z, core), head: 8 (over x, y_hi).
Axes of the slice: x: 4, y: 4 (y_hi: 2, y_lo: 2; y = y_hi * 2 + y_lo), z: 16, core: 2. Of those that a mesh axis runs over, the one named last changes fastest.
Arguments:
- queries: bfloat16 [65536, 2048], P(('seq', 'head')), may hold values from -6 to 6
- keys: bfloat16 [65536, 2048], P(('seq', 'head')), may hold values from -6 to 6
- values: bfloat16 [65536, 2048], P(('seq', 'head')), may hold values from -6 to 6
- out_grad: bfloat16 [65536, 3072], P(('seq', 'head')), may hold values from -24 to 24
- out_weight: bfloat16 [3072, 2048], P('seq', 'head'), may hold values from -0.125 to 0.125
Outputs:
- query_grad: bfloat16 [65536, 2048], P(('seq', 'head'))
- key_grad: bfloat16 [65536, 2048], P(('seq', 'head'))
- value_grad: bfloat16 [65536, 2048], P(('seq', 'head'))
- weight_grad: float32 [3072, 2048], P('seq', 'head')
The draws below stay inside these ranges and needn't reach their ends.
All inputs are finite; a program needn't handle non-finite values.
Results may differ from the reference program's by a relative error of at most 0.039.
Values may be sent and summed in bfloat16 or wider, within the bound.
No kernel may reach another device: no remote copies, remote signals or barrier semaphores. Data moves between devices by JAX's collectives and lax.ppermute only.
A program may use at most 128 MiB of HBM per device.

```python
import math
import jax
import jax.numpy as jnp
from jax import lax

D = 3072
HEADS = 16
HEAD_DIM = 128
TILE = 256
TOKENS = 65536


def draw_queries(key, part):
    key = jax.random.fold_in(key, 1)
    base = jnp.clip(jax.random.normal(key, (TOKENS, HEADS * HEAD_DIM), jnp.float32), -6.0, 6.0)
    return base.astype(jnp.bfloat16)


def draw_keys(key, part):
    key = jax.random.fold_in(key, 2)
    base = jnp.clip(jax.random.normal(key, (TOKENS, HEADS * HEAD_DIM), jnp.float32), -6.0, 6.0)
    return base.astype(jnp.bfloat16)


def raised(entries, own_key, source, target, shards_of, factor):
    def block_of(position):
        return (jnp.arange(entries.shape[position]) // (entries.shape[position] // shards_of)).reshape((-1,) + (1,) * (entries.ndim - 1 - position))

    first = jax.random.permutation(own_key, shards_of)[block_of(target)]
    other_side = (block_of(target) + shards_of // 2) % shards_of
    return jnp.where((block_of(source) == first) | (block_of(source) == other_side), factor * entries, entries)


def steps_of(own_key, extent, cuts, low, top_value):
    gain = 1.0
    for dim, shards_of in cuts:
        steps = jax.random.uniform(jax.random.fold_in(jax.random.fold_in(own_key, 6), dim), (shards_of,), jnp.float32, low / len(cuts), top_value / len(cuts))
        gain = gain * jnp.repeat(jnp.exp(steps), extent[dim] // shards_of).reshape((-1,) + (1,) * (len(extent) - 1 - dim))
    return gain


def normal_values(stream_key, shape, deviation, bound, split=(), kind=jnp.bfloat16):
    loudness = steps_of(stream_key, shape, split, -0.22, 0.18) if split else 1.0
    array = jax.random.normal(stream_key, shape, jnp.float32) * deviation * loudness
    return jnp.minimum(jnp.maximum(array, -bound), bound).astype(kind)


def heavy_noise(stream_key, dims, spread, most, shards, heavy, held_as=jnp.bfloat16):
    array = spread * jax.random.normal(stream_key, dims, jnp.float32)
    if shards:
        array = array * steps_of(stream_key, dims, shards, -0.22, 0.18)
    return jnp.clip(raised(array, jax.random.fold_in(stream_key, 3), *heavy), -most, most).astype(held_as)


def setup_inputs(seed: int = 0) -> dict:
    key_list = jax.random.split(jax.random.key(seed), 6)
    queries = draw_queries(jax.random.fold_in(key_list[5], 71), 0)
    keys = draw_keys(jax.random.fold_in(key_list[5], 71), 0)
    values = normal_values(key_list[2], (TOKENS, HEADS * HEAD_DIM), 1.0, 6.0, ((0, 512),))
    out_grad = heavy_noise(key_list[3], (TOKENS, D), 1.0, 24.0, ((0, 512),), (0, 1, 512, 6.0))
    out_weight = normal_values(key_list[4], (D, HEADS * HEAD_DIM), (HEADS * HEAD_DIM) ** -0.5, 0.125, ((0, 64), (1, 8)))
    return dict(queries=queries, keys=keys, values=values, out_grad=out_grad, out_weight=out_weight)


def reference(queries, keys, values, out_grad, out_weight):
    feat_width = HEADS * HEAD_DIM
    score_scale = 1.0 / math.sqrt(HEAD_DIM)
    span_rows = 3 * TILE
    tile_count = TOKENS // TILE
    highest = lax.Precision.HIGHEST
    dout_full = jnp.dot(out_grad, out_weight, preferred_element_type=jnp.float32).astype(jnp.bfloat16)
    padding = jnp.zeros((TILE, feat_width), jnp.bfloat16)
    keys_pad = jnp.concatenate([padding, keys, padding], axis=0)
    values_pad = jnp.concatenate([padding, values, padding], axis=0)

    def block_step(carry, tile_index):
        dk_acc, dv_acc = carry
        first_row = (tile_index * TILE).astype(jnp.int32)
        query_heads = lax.dynamic_slice_in_dim(queries, first_row, TILE, 0).astype(jnp.float32).reshape(TILE, HEADS, HEAD_DIM)
        dout_heads = lax.dynamic_slice_in_dim(dout_full, first_row, TILE, 0).astype(jnp.float32).reshape(TILE, HEADS, HEAD_DIM)
        key_heads = lax.dynamic_slice_in_dim(keys_pad, first_row, span_rows, 0).astype(jnp.float32).reshape(span_rows, HEADS, HEAD_DIM)
        value_heads = lax.dynamic_slice_in_dim(values_pad, first_row, span_rows, 0).astype(jnp.float32).reshape(span_rows, HEADS, HEAD_DIM)
        key_tile = tile_index - 1 + jnp.arange(span_rows, dtype=jnp.int32) // TILE
        in_window = jnp.logical_and(key_tile >= 0, key_tile < tile_count)
        scores = jnp.einsum('qhd,khd->hqk', query_heads, key_heads, precision=highest) * score_scale
        scores = jnp.where(in_window[None, None, :], scores, -jnp.inf)
        row_top = lax.optimization_barrier(jnp.max(scores, axis=2, keepdims=True))
        log_total = row_top + jnp.log(lax.optimization_barrier(jnp.sum(jnp.exp(scores - row_top), axis=2, keepdims=True)))
        attend = jnp.exp(scores - log_total)
        weights = lax.optimization_barrier(attend.astype(jnp.bfloat16)).astype(jnp.float32)
        attn_heads = jnp.einsum('hqk,khd->qhd', weights, value_heads, precision=highest)
        attn_rows = attn_heads.reshape(TILE, feat_width).astype(jnp.bfloat16)
        attn_back = lax.optimization_barrier(attn_rows).astype(jnp.float32).reshape(TILE, HEADS, HEAD_DIM)
        row_delta = lax.optimization_barrier(jnp.sum(dout_heads * attn_back, axis=2)).T[:, :, None]
        dprobs = jnp.einsum('qhd,khd->hqk', dout_heads, value_heads, precision=highest)
        dscore = (score_scale * attend * (dprobs - row_delta)).astype(jnp.bfloat16)
        dscore = lax.optimization_barrier(dscore).astype(jnp.float32)
        dq_rows = jnp.einsum('hqk,khd->qhd', dscore, key_heads, precision=highest).reshape(TILE, feat_width)
        dk_rows = jnp.einsum('hqk,qhd->khd', dscore, query_heads, precision=highest).reshape(span_rows, feat_width)
        dv_rows = jnp.einsum('hqk,qhd->khd', weights, dout_heads, precision=highest).reshape(span_rows, feat_width)
        dk_acc = lax.dynamic_update_slice_in_dim(dk_acc, lax.dynamic_slice_in_dim(dk_acc, first_row, span_rows, 0) + dk_rows, first_row, 0)
        dv_acc = lax.dynamic_update_slice_in_dim(dv_acc, lax.dynamic_slice_in_dim(dv_acc, first_row, span_rows, 0) + dv_rows, first_row, 0)
        return ((dk_acc, dv_acc), (dq_rows.astype(jnp.bfloat16), attn_rows))
    zero_acc = jnp.zeros((TOKENS + 2 * TILE, feat_width), jnp.float32)
    (dk_acc, dv_acc), (dq_blocks, attn_blocks) = lax.scan(block_step, (zero_acc, zero_acc), jnp.arange(tile_count, dtype=jnp.int32))
    query_grad = dq_blocks.reshape(TOKENS, feat_width)
    key_grad = dk_acc[TILE:TILE + TOKENS].astype(jnp.bfloat16)
    value_grad = dv_acc[TILE:TILE + TOKENS].astype(jnp.bfloat16)
    attn_all = attn_blocks.reshape(TOKENS, feat_width)
    weight_grad = jnp.dot(out_grad.T, attn_all, preferred_element_type=jnp.float32)
    return (query_grad, key_grad, value_grad, weight_grad)
```

```python
import math

import jax
import jax.numpy as jnp
from jax import lax
from jax.experimental import pallas as pl
from jax.experimental.pallas import tpu as pltpu
from jax.sharding import Mesh, PartitionSpec as P

HEAD_DIM = 128
TILE = 256
SCALE = 1.0 / math.sqrt(HEAD_DIM)
F32 = jnp.float32
BF16 = jnp.bfloat16
SEQ = ("ylo", "z", "core")
HEAD = ("x", "yhi")
NT = (((1,), (1,)), ((), ()))
TN = (((0,), (0,)), ((), ()))


def tile_of(ref, u, before, after, count):
    if u < 0:
        return before[...]
    if u >= count:
        return after[...]
    return ref[u * TILE : (u + 1) * TILE, :]


def forward_kernel(bias, q, k, v, kb, vb, ka, va, attn, pt):
    count = q.shape[0] // TILE
    for t in range(count):
        rows = slice(t * TILE, (t + 1) * TILE)
        q_t = q[rows, :]
        parts = []
        for j in range(3):
            u = t + j - 1
            s = lax.dot_general(
                tile_of(k, u, kb, ka, count), q_t, NT, preferred_element_type=F32
            )
            if u < 0:
                s = s + bias[0]
            if u >= count:
                s = s + bias[1]
            parts.append(s)
        top = jnp.maximum(jnp.maximum(parts[0], parts[1]), parts[2])
        top = jnp.max(top, axis=0, keepdims=True)
        parts = [jnp.exp((s - top) * SCALE) for s in parts]
        total = jnp.sum(parts[0] + parts[1] + parts[2], axis=0, keepdims=True)
        inverse = 1.0 / total
        out = jnp.zeros((TILE, HEAD_DIM), F32)
        for j in range(3):
            w = (parts[j] * inverse).astype(BF16)
            pt[0, t, j * TILE : (j + 1) * TILE, :] = w
            out += lax.dot_general(
                w, tile_of(v, t + j - 1, vb, va, count), TN, preferred_element_type=F32
            )
        attn[rows, :] = out.astype(BF16)


def backward_kernel(q, k, v, kb, vb, ka, va, pt, keep, recv, dx, hb, ha):
    count = q.shape[0] // TILE
    h = pl.program_id(0)
    width = 2 * HEAD_DIM
    dk = [jnp.zeros((TILE, HEAD_DIM), F32) for _ in range(count + 2)]
    dv = [jnp.zeros((TILE, HEAD_DIM), F32) for _ in range(count + 2)]
    col = [pl.ds(pl.multiple_of(n * width + h * HEAD_DIM, HEAD_DIM), HEAD_DIM) for n in range(3)]
    for t in range(count):
        rows = slice(t * TILE, (t + 1) * TILE)
        q_t = q[rows, :]
        do = (keep[rows, :] + recv[rows, :].astype(F32)).astype(BF16)
        dps, ws = [], []
        delta = jnp.zeros((1, TILE), F32)
        for j in range(3):
            dp = lax.dot_general(
                tile_of(v, t + j - 1, vb, va, count), do, NT, preferred_element_type=F32
            )
            w = pt[0, t, j * TILE : (j + 1) * TILE, :]
            delta += jnp.sum(w.astype(F32) * dp, axis=0, keepdims=True)
            dps.append(dp)
            ws.append(w)
        dq = jnp.zeros((TILE, HEAD_DIM), F32)
        for j in range(3):
            ds = (ws[j].astype(F32) * (dps[j] - delta)).astype(BF16)
            dv[t + j] += jnp.dot(ws[j], do, preferred_element_type=F32)
            dk[t + j] += jnp.dot(ds, q_t, preferred_element_type=F32)
            dq += lax.dot_general(
                ds, tile_of(k, t + j - 1, kb, ka, count), TN, preferred_element_type=F32
            )
        dx[rows, col[0]] = (dq * SCALE).astype(BF16)
    for u in range(count + 2):
        a = (dk[u] * SCALE).astype(BF16)
        b = dv[u].astype(BF16)
        if u == 0:
            hb[:, col[0]] = a
            hb[:, col[1]] = b
        elif u == count + 1:
            ha[:, col[0]] = a
            ha[:, col[1]] = b
        else:
            rows = slice((u - 1) * TILE, u * TILE)
            dx[rows, col[1]] = a
            dx[rows, col[2]] = b


def column(rows, offset):
    return pl.BlockSpec((rows, HEAD_DIM), lambda h: (0, offset + h))


def tile_specs(rows):
    return [
        column(rows, 0),
        column(rows, 2),
        column(rows, 4),
        column(TILE, 0),
        column(TILE, 2),
        column(TILE, 0),
        column(TILE, 2),
    ]


def attention_forward(bias, x, before, after):
    rows = x.shape[0]
    count = rows // TILE
    return pl.pallas_call(
        forward_kernel,
        grid=(2,),
        in_specs=[pl.BlockSpec(memory_space=pltpu.SMEM)] + tile_specs(rows),
        out_specs=[
            column(rows, 0),
            pl.BlockSpec((1, count, 3 * TILE, TILE), lambda h: (h, 0, 0, 0)),
        ],
        out_shape=[
            jax.ShapeDtypeStruct((rows, 2 * HEAD_DIM), BF16),
            jax.ShapeDtypeStruct((2, count, 3 * TILE, TILE), BF16),
        ],
        compiler_params=pltpu.CompilerParams(vmem_limit_bytes=40 * 1024 * 1024),
        cost_estimate=pl.CostEstimate(
            flops=2 * 2 * 2 * rows * 3 * TILE * HEAD_DIM,
            bytes_accessed=6 * 1024 * 1024,
            transcendentals=2 * rows * 3 * TILE,
        ),
        name="forward",
    )(bias, x, x, x, before, before, after, after)


def attention_backward(x, before, after, pt, keep, recv):
    rows = x.shape[0]
    count = rows // TILE
    return pl.pallas_call(
        backward_kernel,
        grid=(2,),
        in_specs=tile_specs(rows)
        + [
            pl.BlockSpec((1, count, 3 * TILE, TILE), lambda h: (h, 0, 0, 0)),
            column(rows, 0),
            column(rows, 0),
        ],
        out_specs=[
            pl.BlockSpec((rows, 6 * HEAD_DIM), lambda h: (0, 0)),
            pl.BlockSpec((TILE, 4 * HEAD_DIM), lambda h: (0, 0)),
            pl.BlockSpec((TILE, 4 * HEAD_DIM), lambda h: (0, 0)),
        ],
        out_shape=[
            jax.ShapeDtypeStruct((rows, 6 * HEAD_DIM), BF16),
            jax.ShapeDtypeStruct((TILE, 4 * HEAD_DIM), BF16),
            jax.ShapeDtypeStruct((TILE, 4 * HEAD_DIM), BF16),
        ],
        compiler_params=pltpu.CompilerParams(vmem_limit_bytes=40 * 1024 * 1024),
        cost_estimate=pl.CostEstimate(
            flops=2 * 4 * 2 * rows * 3 * TILE * HEAD_DIM,
            bytes_accessed=9 * 1024 * 1024,
            transcendentals=0,
        ),
        name="backward",
    )(x, x, x, before, before, after, after, pt, keep, recv)


def swapped(array, axis):
    return lax.ppermute(array, axis, [(0, 1), (1, 0)])


def crossed(array):
    return lax.ppermute(array, ("ylo", "yhi"), [(0, 0), (1, 2), (2, 1), (3, 3)])


def to_neighbours(down_part, up_part):
    count = lax.axis_size(SEQ)
    up = [(i, i + 1) for i in range(count - 1)]
    down = [(j, i) for i, j in up]
    return lax.ppermute(up_part, SEQ, up), lax.ppermute(down_part, SEQ, down)


def gathered_along_z(array):
    size = lax.axis_size("z")
    place = lax.axis_index("z")
    held = array[None]
    step = size // 2
    while step >= 1:
        other = lax.ppermute(held, "z", [(i, i ^ step) for i in range(size)])
        low = (place // step) % 2 == 0
        first = jnp.where(low, held, other)
        second = jnp.where(low, other, held)
        held = jnp.stack([first, second], axis=1).reshape((-1,) + array.shape)
        step //= 2
    return held


def per_device(queries, keys, values, out_grad, out_weight):
    ylo, core, yhi = (lax.axis_index(a) for a in ("ylo", "core", "yhi"))
    z_count = lax.axis_size("z")
    place = lax.axis_index(SEQ)
    groups = lax.axis_size(HEAD)
    across = lax.axis_size("x")
    width = 2 * HEAD_DIM
    rows_own = queries.shape[0]
    half = out_grad.shape[1] // 2

    packed = jnp.concatenate(
        [a.reshape(rows_own, groups, width) for a in (queries, keys, values)], axis=2
    ).transpose(1, 0, 2)
    x = lax.all_to_all(packed, HEAD, 0, 0, tiled=True).reshape(-1, 3 * width)
    rows = x.shape[0]

    w_part = gathered_along_z(crossed(out_weight))
    w_other = swapped(w_part, "ylo")
    own_is_low = core == 0
    w_pair = jnp.concatenate([w_part, w_other], axis=2)
    w_pair_other = swapped(w_pair, "core")
    w_first = jnp.where(own_is_low, w_pair, w_pair_other)
    w_second = jnp.where(own_is_low, w_pair_other, w_pair)
    w_all = jnp.stack([w_first, w_second], axis=1).reshape(half, 2 * width)
    same = ylo == yhi
    w_keep = jnp.where(same, w_all[:, :width], w_all[:, width:])
    w_send = jnp.where(same, w_all[:, width:], w_all[:, :width])

    og_keep = lax.dynamic_slice_in_dim(out_grad, yhi * half, half, 1)
    og_send = lax.dynamic_slice_in_dim(out_grad, (1 - yhi) * half, half, 1)
    og_other = swapped(og_send, "yhi")
    og_rows = jnp.concatenate(
        [jnp.where(yhi == 0, og_keep, og_other), jnp.where(yhi == 0, og_other, og_keep)], axis=0
    )
    og = lax.all_to_all(
        jnp.broadcast_to(og_rows[None], (across,) + og_rows.shape), "x", 0, 0, tiled=True
    ).reshape(rows, half)

    before, after = to_neighbours(x[:TILE, width:], x[rows - TILE :, width:])
    edge = jnp.stack([place == 0, place == lax.axis_size(SEQ) - 1])
    bias = jnp.where(edge, -1e30, 0.0).astype(F32)
    attn, pt = attention_forward(bias, x, before, after)
    attn_other = swapped(attn, "yhi")

    dout_send = jnp.dot(og, w_send, preferred_element_type=F32).astype(BF16)
    dout_recv = swapped(dout_send, "yhi")
    dout_keep = jnp.dot(og, w_keep, preferred_element_type=F32)

    attn_all = jnp.concatenate(
        [jnp.where(yhi == 0, attn, attn_other), jnp.where(yhi == 0, attn_other, attn)], axis=1
    )
    grad = lax.dot_general(og, attn_all, TN, preferred_element_type=F32)
    grad = grad.reshape(z_count, 2, -1, 2 * width)
    mine = lax.dynamic_index_in_dim(grad, core, 1, keepdims=False)
    other = lax.dynamic_index_in_dim(grad, 1 - core, 1, keepdims=False)
    grad = mine + swapped(other.astype(BF16), "core").astype(F32)
    mine = lax.dynamic_slice_in_dim(grad, ylo * width, width, 2)
    other = lax.dynamic_slice_in_dim(grad, (1 - ylo) * width, width, 2)
    grad = mine + swapped(other.astype(BF16), "ylo").astype(F32)
    grad = lax.all_to_all(grad.astype(BF16), "z", 0, 0, tiled=True)
    weight_grad = crossed(jnp.sum(grad.astype(F32), axis=0))

    dx, dx_before, dx_after = attention_backward(x, before, after, pt, dout_keep, dout_recv)
    from_left, from_right = to_neighbours(dx_before, dx_after)
    dx = dx.at[:TILE, width:].add(from_left)
    dx = dx.at[rows - TILE :, width:].add(from_right)
    dx = lax.all_to_all(dx.reshape(groups, rows_own, 3 * width), HEAD, 0, 0, tiled=True)
    dx = dx.transpose(1, 0, 2).reshape(rows_own, groups, 3, width)
    grads = [dx[:, :, n].reshape(rows_own, groups * width) for n in range(3)]
    return (*grads, weight_grad)


def solution(mesh):
    sizes = (2, mesh.shape["seq"] // 4, 2, mesh.shape["head"] // 2, 2)
    fine = Mesh(mesh.devices.reshape(sizes), ("ylo", "z", "core", "x", "yhi"))
    tokens = P((*SEQ, *HEAD), None)
    weight = P(SEQ, HEAD)
    return jax.shard_map(
        per_device,
        mesh=fine,
        in_specs=(tokens, tokens, tokens, tokens, weight),
        out_specs=(tokens, tokens, tokens, weight),
        check_vma=False,
    )
```

```python
import math

import jax
import jax.numpy as jnp
from jax import lax
from jax.experimental import pallas as pl
from jax.experimental.pallas import tpu as pltpu
from jax.sharding import Mesh, PartitionSpec as P

HEAD_DIM = 128
TILE = 256
SCALE = 1.0 / math.sqrt(HEAD_DIM)
F32 = jnp.float32
BF16 = jnp.bfloat16
SEQ = ("ylo", "z", "core")
HEAD = ("x", "yhi")
NT = (((1,), (1,)), ((), ()))
TN = (((0,), (0,)), ((), ()))


def tile_of(ref, u, before, after, count):
    if u < 0:
        return before[...]
    if u >= count:
        return after[...]
    return ref[u * TILE : (u + 1) * TILE, :]


def forward_kernel(bias, q, k, v, kb, vb, ka, va, attn, pt):
    count = q.shape[0] // TILE
    for t in range(count):
        rows = slice(t * TILE, (t + 1) * TILE)
        q_t = q[rows, :]
        parts = []
        for j in range(3):
            u = t + j - 1
            s = lax.dot_general(
                tile_of(k, u, kb, ka, count), q_t, NT, preferred_element_type=F32
            )
            if u < 0:
                s = s + bias[0]
            if u >= count:
                s = s + bias[1]
            parts.append(s)
        top = jnp.maximum(jnp.maximum(parts[0], parts[1]), parts[2])
        top = jnp.max(top, axis=0, keepdims=True)
        parts = [jnp.exp((s - top) * SCALE) for s in parts]
        total = jnp.sum(parts[0] + parts[1] + parts[2], axis=0, keepdims=True)
        inverse = 1.0 / total
        out = jnp.zeros((TILE, HEAD_DIM), F32)
        for j in range(3):
            w = (parts[j] * inverse).astype(BF16)
            pt[0, t, j * TILE : (j + 1) * TILE, :] = w
            out += lax.dot_general(
                w, tile_of(v, t + j - 1, vb, va, count), TN, preferred_element_type=F32
            )
        attn[rows, :] = out.astype(BF16)


def backward_kernel(q, k, v, kb, vb, ka, va, pt, keep, recv, dx, hb, ha):
    count = q.shape[0] // TILE
    h = pl.program_id(0)
    width = 2 * HEAD_DIM
    dk = [jnp.zeros((TILE, HEAD_DIM), F32) for _ in range(count + 2)]
    dv = [jnp.zeros((TILE, HEAD_DIM), F32) for _ in range(count + 2)]
    col = [pl.ds(pl.multiple_of(n * width + h * HEAD_DIM, HEAD_DIM), HEAD_DIM) for n in range(3)]
    for t in range(count):
        rows = slice(t * TILE, (t + 1) * TILE)
        q_t = q[rows, :]
        do = (keep[rows, :] + recv[rows, :].astype(F32)).astype(BF16)
        dps, ws = [], []
        delta = jnp.zeros((1, TILE), F32)
        for j in range(3):
            dp = lax.dot_general(
                tile_of(v, t + j - 1, vb, va, count), do, NT, preferred_element_type=F32
            )
            w = pt[0, t, j * TILE : (j + 1) * TILE, :]
            delta += jnp.sum(w.astype(F32) * dp, axis=0, keepdims=True)
            dps.append(dp)
            ws.append(w)
        dq = jnp.zeros((TILE, HEAD_DIM), F32)
        for j in range(3):
            ds = (ws[j].astype(F32) * (dps[j] - delta)).astype(BF16)
            dv[t + j] += jnp.dot(ws[j], do, preferred_element_type=F32)
            dk[t + j] += jnp.dot(ds, q_t, preferred_element_type=F32)
            dq += lax.dot_general(
                ds, tile_of(k, t + j - 1, kb, ka, count), TN, preferred_element_type=F32
            )
        dx[rows, col[0]] = (dq * SCALE).astype(BF16)
    for u in range(count + 2):
        a = (dk[u] * SCALE).astype(BF16)
        b = dv[u].astype(BF16)
        if u == 0:
            hb[:, col[0]] = a
            hb[:, col[1]] = b
        elif u == count + 1:
            ha[:, col[0]] = a
            ha[:, col[1]] = b
        else:
            rows = slice((u - 1) * TILE, u * TILE)
            dx[rows, col[1]] = a
            dx[rows, col[2]] = b


def column(rows, offset):
    return pl.BlockSpec((rows, HEAD_DIM), lambda h: (0, offset + h))


def tile_specs(rows):
    return [
        column(rows, 0),
        column(rows, 2),
        column(rows, 4),
        column(TILE, 0),
        column(TILE, 2),
        column(TILE, 0),
        column(TILE, 2),
    ]


def attention_forward(bias, x, before, after):
    rows = x.shape[0]
    count = rows // TILE
    return pl.pallas_call(
        forward_kernel,
        grid=(2,),
        in_specs=[pl.BlockSpec(memory_space=pltpu.SMEM)] + tile_specs(rows),
        out_specs=[
            column(rows, 0),
            pl.BlockSpec((1, count, 3 * TILE, TILE), lambda h: (h, 0, 0, 0)),
        ],
        out_shape=[
            jax.ShapeDtypeStruct((rows, 2 * HEAD_DIM), BF16),
            jax.ShapeDtypeStruct((2, count, 3 * TILE, TILE), BF16),
        ],
        compiler_params=pltpu.CompilerParams(vmem_limit_bytes=40 * 1024 * 1024),
        cost_estimate=pl.CostEstimate(
            flops=2 * 2 * 2 * rows * 3 * TILE * HEAD_DIM,
            bytes_accessed=6 * 1024 * 1024,
            transcendentals=2 * rows * 3 * TILE,
        ),
        name="forward",
    )(bias, x, x, x, before, before, after, after)


def attention_backward(x, before, after, pt, keep, recv):
    rows = x.shape[0]
    count = rows // TILE
    return pl.pallas_call(
        backward_kernel,
        grid=(2,),
        in_specs=tile_specs(rows)
        + [
            pl.BlockSpec((1, count, 3 * TILE, TILE), lambda h: (h, 0, 0, 0)),
            column(rows, 0),
            column(rows, 0),
        ],
        out_specs=[
            pl.BlockSpec((rows, 6 * HEAD_DIM), lambda h: (0, 0)),
            pl.BlockSpec((TILE, 4 * HEAD_DIM), lambda h: (0, 0)),
            pl.BlockSpec((TILE, 4 * HEAD_DIM), lambda h: (0, 0)),
        ],
        out_shape=[
            jax.ShapeDtypeStruct((rows, 6 * HEAD_DIM), BF16),
            jax.ShapeDtypeStruct((TILE, 4 * HEAD_DIM), BF16),
            jax.ShapeDtypeStruct((TILE, 4 * HEAD_DIM), BF16),
        ],
        compiler_params=pltpu.CompilerParams(vmem_limit_bytes=40 * 1024 * 1024),
        cost_estimate=pl.CostEstimate(
            flops=2 * 4 * 2 * rows * 3 * TILE * HEAD_DIM,
            bytes_accessed=9 * 1024 * 1024,
            transcendentals=0,
        ),
        name="backward",
    )(x, x, x, before, before, after, after, pt, keep, recv)


def pack_kernel(q, k, v, out):
    width = 2 * HEAD_DIM
    for g in range(out.shape[0]):
        for n, ref in enumerate((q, k, v)):
            out[g, :, n * width : (n + 1) * width] = ref[:, g * width : (g + 1) * width]


def pack(q, k, v):
    rows, full = q.shape
    width = 2 * HEAD_DIM
    groups = full // width
    part = pl.BlockSpec((rows, 2 * width), lambda i: (0, i))
    return pl.pallas_call(
        pack_kernel,
        grid=(groups // 2,),
        in_specs=[part] * 3,
        out_specs=pl.BlockSpec((2, rows, 3 * width), lambda i: (i, 0, 0)),
        out_shape=jax.ShapeDtypeStruct((groups, rows, 3 * width), BF16),
        cost_estimate=pl.CostEstimate(flops=0, bytes_accessed=3 << 20, transcendentals=0),
        name="pack",
    )(q, k, v)


def unpack_kernel(dx, q, k, v):
    width = 2 * HEAD_DIM
    for g in range(dx.shape[0]):
        for n, ref in enumerate((q, k, v)):
            ref[:, g * width : (g + 1) * width] = dx[g, :, n * width : (n + 1) * width]


def unpack(dx):
    groups, rows, _ = dx.shape
    width = 2 * HEAD_DIM
    part = pl.BlockSpec((rows, 2 * width), lambda i: (0, i))
    return pl.pallas_call(
        unpack_kernel,
        grid=(groups // 2,),
        in_specs=[pl.BlockSpec((2, rows, 3 * width), lambda i: (i, 0, 0))],
        out_specs=[part] * 3,
        out_shape=[jax.ShapeDtypeStruct((rows, groups * width), BF16)] * 3,
        cost_estimate=pl.CostEstimate(flops=0, bytes_accessed=3 << 20, transcendentals=0),
        name="unpack",
    )(dx)


def copies_kernel(yhi, own, other, after, out):
    rows = own.shape[0]
    out[0, pl.ds(pl.multiple_of(yhi[0] * rows, rows), rows), :] = own[...]
    out[0, pl.ds(pl.multiple_of((1 - yhi[0]) * rows, rows), rows), :] = other[...]


def copies(yhi, out_grad, other, after, count):
    rows, half = other.shape
    return pl.pallas_call(
        copies_kernel,
        grid_spec=pltpu.PrefetchScalarGridSpec(
            num_scalar_prefetch=1,
            grid=(count,),
            in_specs=[
                pl.BlockSpec((rows, half), lambda i, y: (0, y[0])),
                pl.BlockSpec((rows, half), lambda i, y: (0, 0)),
                pl.BlockSpec(memory_space=pl.ANY),
            ],
            out_specs=pl.BlockSpec((1, 2 * rows, half), lambda i, y: (i, 0, 0)),
        ),
        out_shape=jax.ShapeDtypeStruct((count, 2 * rows, half), BF16),
        cost_estimate=pl.CostEstimate(flops=0, bytes_accessed=5 << 20, transcendentals=0),
        name="copies",
    )(yhi, out_grad, other, after)


def reversed_bits(value, size):
    bits = size.bit_length() - 1
    out = 0
    for b in range(bits):
        out = out + ((value >> b) & 1) * (1 << (bits - 1 - b))
    return out


def dout_kernel(where, og, own_near, own_far, other_near, other_far, keep, send, weight):
    size, rows, width = own_near.shape

    @pl.when(pl.program_id(0) == 0)
    def _():
        near = pl.ds(pl.multiple_of((1 - where[2]) * width, width), width)
        far = pl.ds(pl.multiple_of(where[2] * width, width), width)
        own = where[1] * rows
        for n in range(size):
            at = reversed_bits(jnp.bitwise_xor(where[0], n), size)
            first = pl.ds(pl.multiple_of(2 * n * rows + own, rows), rows)
            second = pl.ds(pl.multiple_of((2 * n + 1) * rows - own, rows), rows)
            weight[first, near] = own_near[at]
            weight[first, far] = own_far[at]
            weight[second, near] = other_near[at]
            weight[second, far] = other_far[at]

    out = jnp.dot(og[...], weight[...], preferred_element_type=F32)
    keep[...] = out[:, :width]
    send[...] = out[:, width:].astype(BF16)


def dout_parts(where, og, parts):
    rows, half = og.shape
    size, depth, width = parts[0].shape
    block = rows // 4
    whole = pl.BlockSpec((size, depth, width), lambda i, w: (0, 0, 0))
    return pl.pallas_call(
        dout_kernel,
        grid_spec=pltpu.PrefetchScalarGridSpec(
            num_scalar_prefetch=1,
            grid=(4,),
            in_specs=[pl.BlockSpec((block, half), lambda i, w: (i, 0))] + [whole] * 4,
            out_specs=[pl.BlockSpec((block, width), lambda i, w: (i, 0))] * 2,
            scratch_shapes=[pltpu.VMEM((half, 2 * width), BF16)],
        ),
        out_shape=[
            jax.ShapeDtypeStruct((rows, width), F32),
            jax.ShapeDtypeStruct((rows, width), BF16),
        ],
        compiler_params=pltpu.CompilerParams(vmem_limit_bytes=40 * 1024 * 1024),
        cost_estimate=pl.CostEstimate(
            flops=2 * rows * half * 2 * width, bytes_accessed=7 << 20, transcendentals=0
        ),
        name="dout",
    )(where, og, *parts)


def projection_kernel(where, og, attn, attn_other, after, mine, other, total):
    depth = mine.shape[1]
    width = attn.shape[1]
    near = pl.ds(pl.multiple_of((1 - where[2]) * width, width), width)
    far = pl.ds(pl.multiple_of(where[2] * width, width), width)
    total[:, near] = lax.dot_general(og[...], attn[...], TN, preferred_element_type=F32)
    total[:, far] = lax.dot_general(og[...], attn_other[...], TN, preferred_element_type=F32)
    own = where[1] * depth
    for n in range(mine.shape[0]):
        first = pl.ds(pl.multiple_of(2 * n * depth + own, depth), depth)
        second = pl.ds(pl.multiple_of((2 * n + 1) * depth - own, depth), depth)
        mine[n] = total[first, :]
        other[n] = total[second, :].astype(BF16)


def projection_grad(where, og, attn, attn_other, after, size):
    rows, half = og.shape
    width = attn.shape[1]
    depth = half // (2 * size)
    steps = 4
    whole = pl.BlockSpec((rows, width), lambda i, w: (0, 0))
    part = pl.BlockSpec((size // steps, depth, 2 * width), lambda i, w: (i, 0, 0))
    return pl.pallas_call(
        projection_kernel,
        grid_spec=pltpu.PrefetchScalarGridSpec(
            num_scalar_prefetch=1,
            grid=(steps,),
            in_specs=[pl.BlockSpec((rows, half // steps), lambda i, w: (0, i)), whole, whole]
            + [pl.BlockSpec(memory_space=pl.ANY)],
            out_specs=[part, part],
            scratch_shapes=[pltpu.VMEM((half // steps, 2 * width), F32)],
        ),
        out_shape=[
            jax.ShapeDtypeStruct((size, depth, 2 * width), F32),
            jax.ShapeDtypeStruct((size, depth, 2 * width), BF16),
        ],
        compiler_params=pltpu.CompilerParams(vmem_limit_bytes=40 * 1024 * 1024),
        cost_estimate=pl.CostEstimate(
            flops=2 * rows * half * 2 * width, bytes_accessed=7 << 20, transcendentals=0
        ),
        name="projection",
    )(where, og, attn, attn_other, after)


def edges_kernel(dx, low, high, out):
    width = 2 * HEAD_DIM
    out[:, :width] = dx[:, :width]
    added = jnp.where(pl.program_id(0) == 0, low[...].astype(F32), high[...].astype(F32))
    out[:, width:] = (dx[:, width:].astype(F32) + added).astype(BF16)


def add_edges(dx, low, high):
    rows, full = dx.shape
    last = rows // TILE - 1
    part = pl.BlockSpec((TILE, full), lambda i: (i * last, 0))
    edge = pl.BlockSpec(low.shape, lambda i: (0, 0))
    return pl.pallas_call(
        edges_kernel,
        grid=(2,),
        in_specs=[part, edge, edge],
        out_specs=part,
        out_shape=jax.ShapeDtypeStruct(dx.shape, BF16),
        input_output_aliases={0: 0},
        cost_estimate=pl.CostEstimate(flops=0, bytes_accessed=2 << 20, transcendentals=0),
        name="edges",
    )(dx, low, high)


def swapped(array, axis):
    return lax.ppermute(array, axis, [(0, 1), (1, 0)])


Y = ("ylo", "yhi")
FAR = [(2, 0), (1, 3), (0, 1), (3, 2)]
NEAR = [(1, 2), (2, 1)]


def from_owners(block, same):
    far = lax.ppermute(block, Y, [(j, i) for i, j in FAR])
    near = lax.ppermute(block, Y, NEAR)
    return jnp.where(same, block, near), far


def to_owners(near, far, same):
    from_far = lax.ppermute(far.astype(BF16), Y, FAR).astype(F32)
    from_near = lax.ppermute(near.astype(BF16), Y, NEAR).astype(F32)
    return jnp.where(same, near, from_near) + from_far


def to_neighbours(down_part, up_part):
    count = lax.axis_size(SEQ)
    up = [(i, i + 1) for i in range(count - 1)]
    down = [(j, i) for i, j in up]
    return lax.ppermute(up_part, SEQ, up), lax.ppermute(down_part, SEQ, down)


def gathered_along_z(held, steps):
    size = lax.axis_size("z")
    for step in steps:
        other = lax.ppermute(held, "z", [(i, i ^ step) for i in range(size)])
        held = jnp.concatenate([held, other], axis=0)
    return held


def reduced_along_z(array):
    size = lax.axis_size("z")
    place = lax.axis_index("z")
    step = 1
    while step < size:
        halves = array.reshape((-1, 2) + array.shape[1:])
        bit = (place // step) % 2
        own = lax.dynamic_index_in_dim(halves, bit, 1, keepdims=False)
        send = lax.dynamic_index_in_dim(halves, 1 - bit, 1, keepdims=False)
        other = lax.ppermute(send.astype(BF16), "z", [(i, i ^ step) for i in range(size)])
        array = own + other.astype(F32)
        step *= 2
    return array[0]


def per_device(queries, keys, values, out_grad, out_weight):
    ylo, z, core, yhi = (lax.axis_index(a) for a in ("ylo", "z", "core", "yhi"))
    z_count = lax.axis_size("z")
    place = lax.axis_index(SEQ)
    groups = lax.axis_size(HEAD)
    across = lax.axis_size("x")
    width = 2 * HEAD_DIM
    rows_own = queries.shape[0]
    half = out_grad.shape[1] // 2
    same = ylo == yhi
    where = jnp.stack([z, core, same.astype(jnp.int32)]).astype(jnp.int32)

    x = lax.all_to_all(pack(queries, keys, values), HEAD, 0, 0, tiled=True)
    x = x.reshape(-1, 3 * width)
    rows = x.shape[0]

    steps = [z_count >> (n + 1) for n in range(z_count.bit_length() - 1)]
    blocks = gathered_along_z(out_weight[None], steps[:3])

    og_send = lax.dynamic_slice_in_dim(out_grad, (1 - yhi) * half, half, 1)
    og_other = swapped(og_send, "yhi")
    sent = copies(yhi[None].astype(jnp.int32), out_grad, og_other, blocks, across)
    og = lax.all_to_all(sent, "x", 0, 0, tiled=True).reshape(rows, half)

    own_near, own_far = from_owners(gathered_along_z(blocks, steps[3:]), same)
    other_near = swapped(own_near, "core")
    other_far = swapped(own_far, "core")

    before, after = to_neighbours(x[:TILE, width:], x[rows - TILE :, width:])
    edge = jnp.stack([place == 0, place == lax.axis_size(SEQ) - 1])
    bias = jnp.where(edge, -1e30, 0.0).astype(F32)
    attn, pt = attention_forward(bias, x, before, after)
    attn_other = swapped(attn, "yhi")

    dout_keep, dout_send = dout_parts(where, og, (own_near, own_far, other_near, other_far))
    dout_recv = swapped(dout_send, "yhi")

    mine, other = projection_grad(where, og, attn, attn_other, dout_send, z_count)
    grad = mine + swapped(other, "core").astype(F32)
    weight_grad = reduced_along_z(to_owners(grad[:, :, :width], grad[:, :, width:], same))

    dx, dx_before, dx_after = attention_backward(x, before, after, pt, dout_keep, dout_recv)
    from_left, from_right = to_neighbours(dx_before, dx_after)
    dx = add_edges(dx, from_left, from_right)
    dx = lax.all_to_all(dx.reshape(groups, rows_own, 3 * width), HEAD, 0, 0, tiled=True)
    return (*unpack(dx), weight_grad)


def solution(mesh):
    sizes = (2, mesh.shape["seq"] // 4, 2, mesh.shape["head"] // 2, 2)
    fine = Mesh(mesh.devices.reshape(sizes), ("ylo", "z", "core", "x", "yhi"))
    tokens = P((*SEQ, *HEAD), None)
    weight = P(SEQ, HEAD)
    return jax.shard_map(
        per_device,
        mesh=fine,
        in_specs=(tokens, tokens, tokens, tokens, weight),
        out_specs=(tokens, tokens, tokens, weight),
        check_vma=False,
    )
```

```python
import math

import jax
import jax.numpy as jnp
from jax import lax
from jax.experimental import pallas as pl
from jax.experimental.pallas import tpu as pltpu
from jax.sharding import Mesh, PartitionSpec as P

HEAD_DIM = 128
TILE = 256
SCALE = 1.0 / math.sqrt(HEAD_DIM)
F32 = jnp.float32
BF16 = jnp.bfloat16
SEQ = ("ylo", "z", "core")
HEAD = ("x", "yhi")
NT = (((1,), (1,)), ((), ()))
TN = (((0,), (0,)), ((), ()))


def tile_of(ref, u, before, after, count):
    if u < 0:
        return before[...]
    if u >= count:
        return after[...]
    return ref[u * TILE : (u + 1) * TILE, :]


def forward_kernel(bias, q, k, v, kb, vb, ka, va, attn, pt):
    count = q.shape[0] // TILE
    for t in range(count):
        rows = slice(t * TILE, (t + 1) * TILE)
        q_t = q[rows, :]
        parts = []
        for j in range(3):
            u = t + j - 1
            s = lax.dot_general(
                tile_of(k, u, kb, ka, count), q_t, NT, preferred_element_type=F32
            )
            if u < 0:
                s = s + bias[0]
            if u >= count:
                s = s + bias[1]
            parts.append(s)
        top = jnp.maximum(jnp.maximum(parts[0], parts[1]), parts[2])
        top = jnp.max(top, axis=0, keepdims=True)
        parts = [jnp.exp((s - top) * SCALE) for s in parts]
        total = jnp.sum(parts[0] + parts[1] + parts[2], axis=0, keepdims=True)
        inverse = 1.0 / total
        out = jnp.zeros((TILE, HEAD_DIM), F32)
        for j in range(3):
            w = (parts[j] * inverse).astype(BF16)
            pt[0, t, j * TILE : (j + 1) * TILE, :] = w
            out += lax.dot_general(
                w, tile_of(v, t + j - 1, vb, va, count), TN, preferred_element_type=F32
            )
        attn[rows, :] = out.astype(BF16)


def backward_kernel(q, k, v, kb, vb, ka, va, pt, keep, recv, first, dx, hb, ha):
    count = q.shape[0] // TILE
    h = pl.program_id(0)
    width = 2 * HEAD_DIM
    dk = [jnp.zeros((TILE, HEAD_DIM), F32) for _ in range(count + 2)]
    dv = [jnp.zeros((TILE, HEAD_DIM), F32) for _ in range(count + 2)]
    col = [pl.ds(pl.multiple_of(n * width + h * HEAD_DIM, HEAD_DIM), HEAD_DIM) for n in range(3)]
    for t in range(count):
        rows = slice(t * TILE, (t + 1) * TILE)
        q_t = q[rows, :]
        do = (keep[rows, :] + recv[rows, :].astype(F32)).astype(BF16)
        dps, ws = [], []
        delta = jnp.zeros((1, TILE), F32)
        for j in range(3):
            dp = lax.dot_general(
                tile_of(v, t + j - 1, vb, va, count), do, NT, preferred_element_type=F32
            )
            w = pt[0, t, j * TILE : (j + 1) * TILE, :]
            delta += jnp.sum(w.astype(F32) * dp, axis=0, keepdims=True)
            dps.append(dp)
            ws.append(w)
        dq = jnp.zeros((TILE, HEAD_DIM), F32)
        for j in range(3):
            ds = (ws[j].astype(F32) * (dps[j] - delta)).astype(BF16)
            dv[t + j] += jnp.dot(ws[j], do, preferred_element_type=F32)
            dk[t + j] += jnp.dot(ds, q_t, preferred_element_type=F32)
            dq += lax.dot_general(
                ds, tile_of(k, t + j - 1, kb, ka, count), TN, preferred_element_type=F32
            )
        dx[rows, col[0]] = (dq * SCALE).astype(BF16)
    for u in range(count + 2):
        a = (dk[u] * SCALE).astype(BF16)
        b = dv[u].astype(BF16)
        if u == 0:
            hb[:, col[0]] = a
            hb[:, col[1]] = b
        elif u == count + 1:
            ha[:, col[0]] = a
            ha[:, col[1]] = b
        else:
            rows = slice((u - 1) * TILE, u * TILE)
            dx[rows, col[1]] = a
            dx[rows, col[2]] = b


def column(rows, offset):
    return pl.BlockSpec((rows, HEAD_DIM), lambda h: (0, offset + h))


def tile_specs(rows):
    return [
        column(rows, 0),
        column(rows, 2),
        column(rows, 4),
        column(TILE, 0),
        column(TILE, 2),
        column(TILE, 0),
        column(TILE, 2),
    ]


def attention_forward(bias, x, before, after):
    rows = x.shape[0]
    count = rows // TILE
    return pl.pallas_call(
        forward_kernel,
        grid=(2,),
        in_specs=[pl.BlockSpec(memory_space=pltpu.SMEM)] + tile_specs(rows),
        out_specs=[
            column(rows, 0),
            pl.BlockSpec((1, count, 3 * TILE, TILE), lambda h: (h, 0, 0, 0)),
        ],
        out_shape=[
            jax.ShapeDtypeStruct((rows, 2 * HEAD_DIM), BF16),
            jax.ShapeDtypeStruct((2, count, 3 * TILE, TILE), BF16),
        ],
        compiler_params=pltpu.CompilerParams(vmem_limit_bytes=40 * 1024 * 1024),
        cost_estimate=pl.CostEstimate(
            flops=2 * 2 * 2 * rows * 3 * TILE * HEAD_DIM,
            bytes_accessed=6 * 1024 * 1024,
            transcendentals=2 * rows * 3 * TILE,
        ),
        name="forward",
    )(bias, x, x, x, before, before, after, after)


def attention_backward(x, before, after, pt, keep, recv, first):
    rows = x.shape[0]
    count = rows // TILE
    return pl.pallas_call(
        backward_kernel,
        grid=(2,),
        in_specs=tile_specs(rows)
        + [
            pl.BlockSpec((1, count, 3 * TILE, TILE), lambda h: (h, 0, 0, 0)),
            column(rows, 0),
            column(rows, 0),
            pl.BlockSpec(memory_space=pl.ANY),
        ],
        out_specs=[
            pl.BlockSpec((rows, 6 * HEAD_DIM), lambda h: (0, 0)),
            pl.BlockSpec((TILE, 4 * HEAD_DIM), lambda h: (0, 0)),
            pl.BlockSpec((TILE, 4 * HEAD_DIM), lambda h: (0, 0)),
        ],
        out_shape=[
            jax.ShapeDtypeStruct((rows, 6 * HEAD_DIM), BF16),
            jax.ShapeDtypeStruct((TILE, 4 * HEAD_DIM), BF16),
            jax.ShapeDtypeStruct((TILE, 4 * HEAD_DIM), BF16),
        ],
        compiler_params=pltpu.CompilerParams(vmem_limit_bytes=40 * 1024 * 1024),
        cost_estimate=pl.CostEstimate(
            flops=100 * 2 * 4 * 2 * rows * 3 * TILE * HEAD_DIM,
            bytes_accessed=9 * 1024 * 1024,
            transcendentals=0,
        ),
        name="backward",
    )(x, x, x, before, before, after, after, pt, keep, recv, first)


def pack_kernel(q, k, v, out):
    width = 2 * HEAD_DIM
    for g in range(out.shape[0]):
        for n, ref in enumerate((q, k, v)):
            out[g, :, n * width : (n + 1) * width] = ref[:, g * width : (g + 1) * width]


def pack(q, k, v):
    rows, full = q.shape
    width = 2 * HEAD_DIM
    groups = full // width
    part = pl.BlockSpec((rows, 2 * width), lambda i: (0, i))
    return pl.pallas_call(
        pack_kernel,
        grid=(groups // 2,),
        in_specs=[part] * 3,
        out_specs=pl.BlockSpec((2, rows, 3 * width), lambda i: (i, 0, 0)),
        out_shape=jax.ShapeDtypeStruct((groups, rows, 3 * width), BF16),
        cost_estimate=pl.CostEstimate(flops=0, bytes_accessed=3 << 20, transcendentals=0),
        name="pack",
    )(q, k, v)


def dout_kernel(where, og, own, other, first, keep, send, weight):
    size, rows, _ = own.shape
    width = keep.shape[1]

    @pl.when(pl.program_id(0) == 0)
    def _():
        near = pl.ds(pl.multiple_of((1 - where[1]) * width, width), width)
        far = pl.ds(pl.multiple_of(where[1] * width, width), width)
        for n in range(size):
            for ref, place in ((own, where[0]), (other, 1 - where[0])):
                to = pl.ds(pl.multiple_of((2 * n + place) * rows, rows), rows)
                weight[to, near] = ref[n, :, :width]
                weight[to, far] = ref[n, :, width:]

    out = jnp.dot(og[...], weight[...], preferred_element_type=F32)
    keep[...] = out[:, :width]
    send[...] = out[:, width:].astype(BF16)


def dout_parts(where, og, own, other, first):
    rows, half = og.shape
    size, depth, both = own.shape
    width = both // 2
    block = rows // 4
    whole = pl.BlockSpec((size, depth, both), lambda i, w: (0, 0, 0))
    return pl.pallas_call(
        dout_kernel,
        grid_spec=pltpu.PrefetchScalarGridSpec(
            num_scalar_prefetch=1,
            grid=(4,),
            in_specs=[pl.BlockSpec((block, half), lambda i, w: (i, 0)), whole, whole]
            + [pl.BlockSpec(memory_space=pl.ANY)],
            out_specs=[pl.BlockSpec((block, width), lambda i, w: (i, 0))] * 2,
            scratch_shapes=[pltpu.VMEM((half, both), BF16)],
        ),
        out_shape=[
            jax.ShapeDtypeStruct((rows, width), F32),
            jax.ShapeDtypeStruct((rows, width), BF16),
        ],
        compiler_params=pltpu.CompilerParams(vmem_limit_bytes=40 * 1024 * 1024),
        cost_estimate=pl.CostEstimate(
            flops=2 * rows * half * both, bytes_accessed=7 << 20, transcendentals=0
        ),
        name="dout",
    )(where, og, own, other, first)


def projection_kernel(where, og, attn, attn_other, first, mine, other, total):
    depth = mine.shape[1]
    width = attn.shape[1]
    near = pl.ds(pl.multiple_of((1 - where[1]) * width, width), width)
    far = pl.ds(pl.multiple_of(where[1] * width, width), width)
    total[:, near] = lax.dot_general(og[...], attn[...], TN, preferred_element_type=F32)
    total[:, far] = lax.dot_general(og[...], attn_other[...], TN, preferred_element_type=F32)
    own = where[0] * depth
    for n in range(mine.shape[0]):
        first = pl.ds(pl.multiple_of(2 * n * depth + own, depth), depth)
        second = pl.ds(pl.multiple_of((2 * n + 1) * depth - own, depth), depth)
        mine[n] = total[first, :]
        other[n] = total[second, :].astype(BF16)


def projection_grad(where, og, attn, attn_other, first, size):
    rows, half = og.shape
    width = attn.shape[1]
    depth = half // (2 * size)
    steps = 4
    whole = pl.BlockSpec((rows, width), lambda i, w: (0, 0))
    part = pl.BlockSpec((size // steps, depth, 2 * width), lambda i, w: (i, 0, 0))
    return pl.pallas_call(
        projection_kernel,
        grid_spec=pltpu.PrefetchScalarGridSpec(
            num_scalar_prefetch=1,
            grid=(steps,),
            in_specs=[pl.BlockSpec((rows, half // steps), lambda i, w: (0, i)), whole, whole]
            + [pl.BlockSpec(memory_space=pl.ANY)],
            out_specs=[part, part],
            scratch_shapes=[pltpu.VMEM((half // steps, 2 * width), F32)],
        ),
        out_shape=[
            jax.ShapeDtypeStruct((size, depth, 2 * width), F32),
            jax.ShapeDtypeStruct((size, depth, 2 * width), BF16),
        ],
        compiler_params=pltpu.CompilerParams(vmem_limit_bytes=40 * 1024 * 1024),
        cost_estimate=pl.CostEstimate(
            flops=2 * rows * half * 2 * width, bytes_accessed=7 << 20, transcendentals=0
        ),
        name="projection",
    )(where, og, attn, attn_other, first)


def edges_kernel(dx, low, high, out):
    width = 2 * HEAD_DIM
    out[:, :width] = dx[:, :width]
    added = jnp.where(pl.program_id(0) == 0, low[...].astype(F32), high[...].astype(F32))
    out[:, width:] = (dx[:, width:].astype(F32) + added).astype(BF16)


def add_edges(dx, low, high):
    rows, full = dx.shape
    last = rows // TILE - 1
    part = pl.BlockSpec((TILE, full), lambda i: (i * last, 0))
    edge = pl.BlockSpec(low.shape, lambda i: (0, 0))
    return pl.pallas_call(
        edges_kernel,
        grid=(2,),
        in_specs=[part, edge, edge],
        out_specs=part,
        out_shape=jax.ShapeDtypeStruct(dx.shape, BF16),
        input_output_aliases={0: 0},
        cost_estimate=pl.CostEstimate(flops=0, bytes_accessed=2 << 20, transcendentals=0),
        name="edges",
    )(dx, low, high)


def tie_kernel(*refs):
    pass


def tie(array, *first):
    spec = pl.BlockSpec(memory_space=pl.ANY)
    return pl.pallas_call(
        tie_kernel,
        in_specs=[spec] * (1 + len(first)),
        out_specs=spec,
        out_shape=jax.ShapeDtypeStruct(array.shape, array.dtype),
        input_output_aliases={0: 0},
        cost_estimate=pl.CostEstimate(flops=0, bytes_accessed=0, transcendentals=0),
        name="tie",
    )(array, *first)


def swapped(array, axis):
    return lax.ppermute(array, axis, [(0, 1), (1, 0)])


Y = ("ylo", "yhi")
FAR = [(2, 0), (1, 3), (0, 1), (3, 2)]
NEAR = [(1, 2), (2, 1)]


def from_owners(block, same):
    far = lax.ppermute(block, Y, [(j, i) for i, j in FAR])
    near = lax.ppermute(block, Y, NEAR)
    return jnp.where(same, block, near), far


def to_neighbours(down_part, up_part):
    count = lax.axis_size(SEQ)
    up = [(i, i + 1) for i in range(count - 1)]
    down = [(j, i) for i, j in up]
    return lax.ppermute(up_part, SEQ, up), lax.ppermute(down_part, SEQ, down)


def reduced_along_z(array):
    size = lax.axis_size("z")
    place = lax.axis_index("z")
    step = 1
    while step < size // 2:
        halves = array.reshape((-1, 2) + array.shape[1:])
        bit = (place // step) % 2
        own = lax.dynamic_index_in_dim(halves, bit, 1, keepdims=False)
        send = lax.dynamic_index_in_dim(halves, 1 - bit, 1, keepdims=False)
        other = lax.ppermute(send.astype(BF16), "z", [(i, i ^ step) for i in range(size)])
        array = own + other.astype(F32)
        step *= 2
    bit = place // step
    own = lax.dynamic_index_in_dim(array, bit, 0, keepdims=False)
    send = lax.dynamic_index_in_dim(array, 1 - bit, 0, keepdims=False)
    axes = ("ylo", "z", "yhi")

    def pairs(flip):
        at = lambda a, z, b: (a * size + z) * 2 + b
        return [
            (at(a, z, b), at(b, z ^ flip, a)) for a in range(2) for z in range(size) for b in range(2)
        ]

    near = lax.ppermute(own, axes, pairs(0))
    far = lax.ppermute(send, axes, pairs(step))
    return near, far


def per_device(queries, keys, values, out_grad, out_weight):
    ylo, core, yhi = (lax.axis_index(a) for a in ("ylo", "core", "yhi"))
    z_count = lax.axis_size("z")
    place = lax.axis_index(SEQ)
    groups = lax.axis_size(HEAD)
    width = 2 * HEAD_DIM
    rows_own = queries.shape[0]
    half = out_grad.shape[1] // 2
    same = ylo == yhi
    where = jnp.stack([core, same]).astype(jnp.int32)

    owned = lax.all_gather(out_weight, "z", axis=0)
    weight = jnp.concatenate(from_owners(owned, same), axis=2)

    og_own = lax.dynamic_slice_in_dim(out_grad, yhi * half, half, 1)
    og_send = lax.dynamic_slice_in_dim(out_grad, (1 - yhi) * half, half, 1)
    og_other = swapped(og_send, "yhi")
    og = jnp.concatenate(
        [jnp.where(yhi == 0, og_own, og_other), jnp.where(yhi == 0, og_other, og_own)], axis=0
    )
    og = jnp.broadcast_to(og[None], (lax.axis_size("x"),) + og.shape)

    x = pack(queries, keys, values)
    x = lax.all_to_all(x, HEAD, 0, 0, tiled=True).reshape(-1, 3 * width)
    rows = x.shape[0]
    before, after = to_neighbours(x[:TILE, width:], x[rows - TILE :, width:])

    og = lax.all_to_all(tie(og, x, owned), "x", 0, 0, tiled=True).reshape(rows, half)

    edge = jnp.stack([place == 0, place == lax.axis_size(SEQ) - 1])
    bias = jnp.where(edge, -1e30, 0.0).astype(F32)
    attn, pt = attention_forward(bias, x, before, after)
    attn_other = swapped(attn, "yhi")
    weight = tie(weight, attn)
    weight_other = swapped(weight, "core")

    mine, other = projection_grad(where, og, attn, attn_other, weight, z_count)
    grad = mine + swapped(other, "core").astype(F32)
    far = grad[:, :, width:].astype(BF16)
    parts = reduced_along_z(grad[:, :, :width] + swapped(far, "ylo").astype(F32))

    dout_keep, dout_send = dout_parts(where, og, weight, weight_other, other)
    dout_recv = swapped(dout_send, "yhi")

    dx, dx_before, dx_after = attention_backward(
        x, before, after, pt, dout_keep, dout_recv, far
    )
    from_left, from_right = to_neighbours(dx_before, dx_after)
    dx = add_edges(dx, from_left, from_right)
    dx = lax.all_to_all(dx.reshape(groups, rows_own, 3 * width), HEAD, 0, 0, tiled=True)
    grads = [
        dx[:, :, n * width : (n + 1) * width].transpose(1, 0, 2).reshape(rows_own, -1)
        for n in range(3)
    ]
    return (*grads, tie(parts[0], grads[0]) + parts[1])


def solution(mesh):
    sizes = (2, mesh.shape["seq"] // 4, 2, mesh.shape["head"] // 2, 2)
    fine = Mesh(mesh.devices.reshape(sizes), ("ylo", "z", "core", "x", "yhi"))
    tokens = P((*SEQ, *HEAD), None)
    weight = P(SEQ, HEAD)
    return jax.shard_map(
        per_device,
        mesh=fine,
        in_specs=(tokens, tokens, tokens, tokens, weight),
        out_specs=(tokens, tokens, tokens, weight),
        check_vma=False,
    )
```

```python
import math

import jax
import jax.numpy as jnp
from jax import lax
from jax.experimental import pallas as pl
from jax.experimental.pallas import tpu as pltpu
from jax.sharding import Mesh, PartitionSpec as P

HEAD_DIM = 128
TILE = 256
SCALE = 1.0 / math.sqrt(HEAD_DIM)
F32 = jnp.float32
BF16 = jnp.bfloat16
SEQ = ("ylo", "z", "core")
HEAD = ("x", "yhi")
NT = (((1,), (1,)), ((), ()))
TN = (((0,), (0,)), ((), ()))


def tile_of(ref, u, before, after, count):
    if u < 0:
        return before[...]
    if u >= count:
        return after[...]
    return ref[u * TILE : (u + 1) * TILE, :]


def forward_kernel(bias, q, k, v, kb, vb, ka, va, attn, pt):
    count = q.shape[0] // TILE
    for t in range(count):
        rows = slice(t * TILE, (t + 1) * TILE)
        q_t = q[rows, :]
        parts = []
        for j in range(3):
            u = t + j - 1
            s = lax.dot_general(
                tile_of(k, u, kb, ka, count), q_t, NT, preferred_element_type=F32
            )
            if u < 0:
                s = s + bias[0]
            if u >= count:
                s = s + bias[1]
            parts.append(s)
        top = jnp.maximum(jnp.maximum(parts[0], parts[1]), parts[2])
        top = jnp.max(top, axis=0, keepdims=True)
        parts = [jnp.exp((s - top) * SCALE) for s in parts]
        total = jnp.sum(parts[0] + parts[1] + parts[2], axis=0, keepdims=True)
        inverse = 1.0 / total
        out = jnp.zeros((TILE, HEAD_DIM), F32)
        for j in range(3):
            w = (parts[j] * inverse).astype(BF16)
            pt[0, t, j * TILE : (j + 1) * TILE, :] = w
            out += lax.dot_general(
                w, tile_of(v, t + j - 1, vb, va, count), TN, preferred_element_type=F32
            )
        attn[rows, :] = out.astype(BF16)


def backward_kernel(q, k, v, kb, vb, ka, va, pt, keep, recv, first, dx, hb, ha):
    count = q.shape[0] // TILE
    h = pl.program_id(0)
    width = 2 * HEAD_DIM
    dk = [jnp.zeros((TILE, HEAD_DIM), F32) for _ in range(count + 2)]
    dv = [jnp.zeros((TILE, HEAD_DIM), F32) for _ in range(count + 2)]
    col = [pl.ds(pl.multiple_of(n * width + h * HEAD_DIM, HEAD_DIM), HEAD_DIM) for n in range(3)]
    for t in range(count):
        rows = slice(t * TILE, (t + 1) * TILE)
        q_t = q[rows, :]
        do = (keep[rows, :] + recv[rows, :].astype(F32)).astype(BF16)
        dps, ws = [], []
        delta = jnp.zeros((1, TILE), F32)
        for j in range(3):
            dp = lax.dot_general(
                tile_of(v, t + j - 1, vb, va, count), do, NT, preferred_element_type=F32
            )
            w = pt[0, t, j * TILE : (j + 1) * TILE, :]
            delta += jnp.sum(w.astype(F32) * dp, axis=0, keepdims=True)
            dps.append(dp)
            ws.append(w)
        dq = jnp.zeros((TILE, HEAD_DIM), F32)
        for j in range(3):
            ds = (ws[j].astype(F32) * (dps[j] - delta)).astype(BF16)
            dv[t + j] += jnp.dot(ws[j], do, preferred_element_type=F32)
            dk[t + j] += jnp.dot(ds, q_t, preferred_element_type=F32)
            dq += lax.dot_general(
                ds, tile_of(k, t + j - 1, kb, ka, count), TN, preferred_element_type=F32
            )
        dx[rows, col[0]] = (dq * SCALE).astype(BF16)
    for u in range(count + 2):
        a = (dk[u] * SCALE).astype(BF16)
        b = dv[u].astype(BF16)
        if u == 0:
            hb[:, col[0]] = a
            hb[:, col[1]] = b
        elif u == count + 1:
            ha[:, col[0]] = a
            ha[:, col[1]] = b
        else:
            rows = slice((u - 1) * TILE, u * TILE)
            dx[rows, col[1]] = a
            dx[rows, col[2]] = b


def column(rows, offset):
    return pl.BlockSpec((rows, HEAD_DIM), lambda h: (0, offset + h))


def tile_specs(rows):
    return [
        column(rows, 0),
        column(rows, 2),
        column(rows, 4),
        column(TILE, 0),
        column(TILE, 2),
        column(TILE, 0),
        column(TILE, 2),
    ]


def attention_forward(bias, x, before, after):
    rows = x.shape[0]
    count = rows // TILE
    return pl.pallas_call(
        forward_kernel,
        grid=(2,),
        in_specs=[pl.BlockSpec(memory_space=pltpu.SMEM)] + tile_specs(rows),
        out_specs=[
            column(rows, 0),
            pl.BlockSpec((1, count, 3 * TILE, TILE), lambda h: (h, 0, 0, 0)),
        ],
        out_shape=[
            jax.ShapeDtypeStruct((rows, 2 * HEAD_DIM), BF16),
            pltpu.HBM((2, count, 3 * TILE, TILE), BF16),
        ],
        compiler_params=pltpu.CompilerParams(vmem_limit_bytes=40 * 1024 * 1024),
        cost_estimate=pl.CostEstimate(
            flops=2 * 2 * 2 * rows * 3 * TILE * HEAD_DIM,
            bytes_accessed=6 * 1024 * 1024,
            transcendentals=2 * rows * 3 * TILE,
        ),
        name="forward",
    )(bias, x, x, x, before, before, after, after)


def attention_backward(x, before, after, pt, keep, recv, first):
    rows = x.shape[0]
    count = rows // TILE
    return pl.pallas_call(
        backward_kernel,
        grid=(2,),
        in_specs=tile_specs(rows)
        + [
            pl.BlockSpec((1, count, 3 * TILE, TILE), lambda h: (h, 0, 0, 0)),
            column(rows, 0),
            column(rows, 0),
            pl.BlockSpec(memory_space=pl.ANY),
        ],
        out_specs=[
            pl.BlockSpec((rows, 6 * HEAD_DIM), lambda h: (0, 0)),
            pl.BlockSpec((TILE, 4 * HEAD_DIM), lambda h: (0, 0)),
            pl.BlockSpec((TILE, 4 * HEAD_DIM), lambda h: (0, 0)),
        ],
        out_shape=[
            pltpu.HBM((rows, 6 * HEAD_DIM), BF16),
            jax.ShapeDtypeStruct((TILE, 4 * HEAD_DIM), BF16),
            jax.ShapeDtypeStruct((TILE, 4 * HEAD_DIM), BF16),
        ],
        compiler_params=pltpu.CompilerParams(vmem_limit_bytes=40 * 1024 * 1024),
        cost_estimate=pl.CostEstimate(
            flops=100 * 2 * 4 * 2 * rows * 3 * TILE * HEAD_DIM,
            bytes_accessed=9 * 1024 * 1024,
            transcendentals=0,
        ),
        name="backward",
    )(x, x, x, before, before, after, after, pt, keep, recv, first)


def pack_kernel(q, k, v, out):
    width = 2 * HEAD_DIM
    for g in range(out.shape[0]):
        for n, ref in enumerate((q, k, v)):
            out[g, :, n * width : (n + 1) * width] = ref[:, g * width : (g + 1) * width]


def pack(q, k, v):
    rows, full = q.shape
    width = 2 * HEAD_DIM
    groups = full // width
    part = pl.BlockSpec((rows, 2 * width), lambda i: (0, i))
    return pl.pallas_call(
        pack_kernel,
        grid=(groups // 2,),
        in_specs=[part] * 3,
        out_specs=pl.BlockSpec((2, rows, 3 * width), lambda i: (i, 0, 0)),
        out_shape=jax.ShapeDtypeStruct((groups, rows, 3 * width), BF16),
        cost_estimate=pl.CostEstimate(flops=0, bytes_accessed=3 << 20, transcendentals=0),
        name="pack",
    )(q, k, v)


def dout_kernel(where, og, own, other, first, keep, send, weight):
    size, rows, _ = own.shape
    width = keep.shape[1]

    @pl.when(pl.program_id(0) == 0)
    def _():
        near = pl.ds(pl.multiple_of((1 - where[1]) * width, width), width)
        far = pl.ds(pl.multiple_of(where[1] * width, width), width)
        for n in range(size):
            for ref, place in ((own, where[0]), (other, 1 - where[0])):
                to = pl.ds(pl.multiple_of((2 * n + place) * rows, rows), rows)
                weight[to, near] = ref[n, :, :width]
                weight[to, far] = ref[n, :, width:]

    out = jnp.dot(og[...], weight[...], preferred_element_type=F32)
    keep[...] = out[:, :width]
    send[...] = out[:, width:].astype(BF16)


def dout_parts(where, og, own, other, first):
    rows, half = og.shape
    size, depth, both = own.shape
    width = both // 2
    block = rows // 4
    whole = pl.BlockSpec((size, depth, both), lambda i, w: (0, 0, 0))
    return pl.pallas_call(
        dout_kernel,
        grid_spec=pltpu.PrefetchScalarGridSpec(
            num_scalar_prefetch=1,
            grid=(4,),
            in_specs=[pl.BlockSpec((block, half), lambda i, w: (i, 0)), whole, whole]
            + [pl.BlockSpec(memory_space=pl.ANY)],
            out_specs=[pl.BlockSpec((block, width), lambda i, w: (i, 0))] * 2,
            scratch_shapes=[pltpu.VMEM((half, both), BF16)],
        ),
        out_shape=[
            pltpu.HBM((rows, width), F32),
            jax.ShapeDtypeStruct((rows, width), BF16),
        ],
        compiler_params=pltpu.CompilerParams(vmem_limit_bytes=40 * 1024 * 1024),
        cost_estimate=pl.CostEstimate(
            flops=2 * rows * half * both, bytes_accessed=7 << 20, transcendentals=0
        ),
        name="dout",
    )(where, og, own, other, first)


def projection_kernel(where, og, attn, attn_other, first, mine, other, total):
    depth = mine.shape[1]
    width = attn.shape[1]
    near = pl.ds(pl.multiple_of((1 - where[1]) * width, width), width)
    far = pl.ds(pl.multiple_of(where[1] * width, width), width)
    total[:, near] = lax.dot_general(og[...], attn[...], TN, preferred_element_type=F32)
    total[:, far] = lax.dot_general(og[...], attn_other[...], TN, preferred_element_type=F32)
    own = where[0] * depth
    for n in range(mine.shape[0]):
        first = pl.ds(pl.multiple_of(2 * n * depth + own, depth), depth)
        second = pl.ds(pl.multiple_of((2 * n + 1) * depth - own, depth), depth)
        mine[n] = total[first, :]
        other[n] = total[second, :].astype(BF16)


def projection_grad(where, og, attn, attn_other, first, size):
    rows, half = og.shape
    width = attn.shape[1]
    depth = half // (2 * size)
    steps = 4
    whole = pl.BlockSpec((rows, width), lambda i, w: (0, 0))
    part = pl.BlockSpec((size // steps, depth, 2 * width), lambda i, w: (i, 0, 0))
    return pl.pallas_call(
        projection_kernel,
        grid_spec=pltpu.PrefetchScalarGridSpec(
            num_scalar_prefetch=1,
            grid=(steps,),
            in_specs=[pl.BlockSpec((rows, half // steps), lambda i, w: (0, i)), whole, whole]
            + [pl.BlockSpec(memory_space=pl.ANY)],
            out_specs=[part, part],
            scratch_shapes=[pltpu.VMEM((half // steps, 2 * width), F32)],
        ),
        out_shape=[
            jax.ShapeDtypeStruct((size, depth, 2 * width), F32),
            jax.ShapeDtypeStruct((size, depth, 2 * width), BF16),
        ],
        compiler_params=pltpu.CompilerParams(vmem_limit_bytes=60 * 1024 * 1024),
        cost_estimate=pl.CostEstimate(
            flops=2 * rows * half * 2 * width, bytes_accessed=7 << 20, transcendentals=0
        ),
        name="projection",
    )(where, og, attn, attn_other, first)


def edges_kernel(dx, low, high, out):
    width = 2 * HEAD_DIM
    out[:, :width] = dx[:, :width]
    added = jnp.where(pl.program_id(0) == 0, low[...].astype(F32), high[...].astype(F32))
    out[:, width:] = (dx[:, width:].astype(F32) + added).astype(BF16)


def add_edges(dx, low, high):
    rows, full = dx.shape
    last = rows // TILE - 1
    part = pl.BlockSpec((TILE, full), lambda i: (i * last, 0))
    edge = pl.BlockSpec(low.shape, lambda i: (0, 0))
    return pl.pallas_call(
        edges_kernel,
        grid=(2,),
        in_specs=[part, edge, edge],
        out_specs=part,
        out_shape=jax.ShapeDtypeStruct(dx.shape, BF16),
        input_output_aliases={0: 0},
        cost_estimate=pl.CostEstimate(flops=0, bytes_accessed=2 << 20, transcendentals=0),
        name="edges",
    )(dx, low, high)


def tie_kernel(*refs):
    pass


def tie(array, *first):
    spec = pl.BlockSpec(memory_space=pl.ANY)
    return pl.pallas_call(
        tie_kernel,
        in_specs=[spec] * (1 + len(first)),
        out_specs=spec,
        out_shape=jax.ShapeDtypeStruct(array.shape, array.dtype),
        input_output_aliases={0: 0},
        cost_estimate=pl.CostEstimate(flops=0, bytes_accessed=0, transcendentals=0),
        name="tie",
    )(array, *first)


def swapped(array, axis):
    return lax.ppermute(array, axis, [(0, 1), (1, 0)])


Y = ("ylo", "yhi")
FAR = [(2, 0), (1, 3), (0, 1), (3, 2)]
NEAR = [(1, 2), (2, 1)]


def from_owners(block, same):
    far = lax.ppermute(block, Y, [(j, i) for i, j in FAR])
    near = lax.ppermute(block, Y, NEAR)
    return jnp.where(same, block, near), far


def to_neighbours(down_part, up_part):
    count = lax.axis_size(SEQ)
    up = [(i, i + 1) for i in range(count - 1)]
    down = [(j, i) for i, j in up]
    return lax.ppermute(up_part, SEQ, up), lax.ppermute(down_part, SEQ, down)


def reduced_along_z(array):
    size = lax.axis_size("z")
    place = lax.axis_index("z")
    step = 1
    while step < size // 2:
        halves = array.reshape((-1, 2) + array.shape[1:])
        bit = (place // step) % 2
        own = lax.dynamic_index_in_dim(halves, bit, 1, keepdims=False)
        send = lax.dynamic_index_in_dim(halves, 1 - bit, 1, keepdims=False)
        other = lax.ppermute(send.astype(BF16), "z", [(i, i ^ step) for i in range(size)])
        array = own + other.astype(F32)
        step *= 2
    bit = place // step
    own = lax.dynamic_index_in_dim(array, bit, 0, keepdims=False)
    send = lax.dynamic_index_in_dim(array, 1 - bit, 0, keepdims=False)
    axes = ("ylo", "z", "yhi")

    def pairs(flip):
        at = lambda a, z, b: (a * size + z) * 2 + b
        return [
            (at(a, z, b), at(b, z ^ flip, a)) for a in range(2) for z in range(size) for b in range(2)
        ]

    near = lax.ppermute(own, axes, pairs(0))
    far = lax.ppermute(send, axes, pairs(step))
    return near, far


def per_device(queries, keys, values, out_grad, out_weight):
    ylo, core, yhi = (lax.axis_index(a) for a in ("ylo", "core", "yhi"))
    z_count = lax.axis_size("z")
    place = lax.axis_index(SEQ)
    groups = lax.axis_size(HEAD)
    width = 2 * HEAD_DIM
    rows_own = queries.shape[0]
    half = out_grad.shape[1] // 2
    same = ylo == yhi
    where = jnp.stack([core, same]).astype(jnp.int32)

    owned = lax.all_gather(out_weight, "z", axis=0)
    weight = jnp.concatenate(from_owners(owned, same), axis=2)

    og_own = lax.dynamic_slice_in_dim(out_grad, yhi * half, half, 1)
    og_send = lax.dynamic_slice_in_dim(out_grad, (1 - yhi) * half, half, 1)
    og_other = swapped(og_send, "yhi")
    og = jnp.concatenate(
        [jnp.where(yhi == 0, og_own, og_other), jnp.where(yhi == 0, og_other, og_own)], axis=0
    )
    og = jnp.broadcast_to(og[None], (lax.axis_size("x"),) + og.shape)

    x = pack(queries, keys, values)
    x = lax.all_to_all(x, HEAD, 0, 0, tiled=True).reshape(-1, 3 * width)
    rows = x.shape[0]
    before, after = to_neighbours(x[:TILE, width:], x[rows - TILE :, width:])

    og = lax.all_to_all(tie(og, x, owned), "x", 0, 0, tiled=True).reshape(rows, half)

    edge = jnp.stack([place == 0, place == lax.axis_size(SEQ) - 1])
    bias = jnp.where(edge, -1e30, 0.0).astype(F32)
    attn, pt = attention_forward(bias, x, before, after)
    attn_other = swapped(attn, "yhi")
    weight = tie(weight, attn)
    weight_other = swapped(weight, "core")

    mine, other = projection_grad(where, og, attn, attn_other, weight, z_count)
    grad = mine + swapped(other, "core").astype(F32)
    far = grad[:, :, width:].astype(BF16)
    parts = reduced_along_z(grad[:, :, :width] + swapped(far, "ylo").astype(F32))

    dout_keep, dout_send = dout_parts(where, og, weight, weight_other, other)
    dout_recv = swapped(dout_send, "yhi")

    dx, dx_before, dx_after = attention_backward(
        x, before, after, pt, dout_keep, dout_recv, far
    )
    from_left, from_right = to_neighbours(dx_before, dx_after)
    dx = add_edges(dx, from_left, from_right)
    dx = lax.all_to_all(dx.reshape(groups, rows_own, 3 * width), HEAD, 0, 0, tiled=True)
    grads = [
        dx[:, :, n * width : (n + 1) * width].transpose(1, 0, 2).reshape(rows_own, -1)
        for n in range(3)
    ]
    return (*grads, tie(parts[0], grads[0]) + parts[1])


def solution(mesh):
    sizes = (2, mesh.shape["seq"] // 4, 2, mesh.shape["head"] // 2, 2)
    fine = Mesh(mesh.devices.reshape(sizes), ("ylo", "z", "core", "x", "yhi"))
    tokens = P((*SEQ, *HEAD), None)
    weight = P(SEQ, HEAD)
    return jax.shard_map(
        per_device,
        mesh=fine,
        in_specs=(tokens, tokens, tokens, tokens, weight),
        out_specs=(tokens, tokens, tokens, weight),
        check_vma=False,
    )
```

```python
import math

import jax
import jax.numpy as jnp
from jax import lax
from jax.experimental import pallas as pl
from jax.experimental.pallas import tpu as pltpu
from jax.sharding import Mesh, PartitionSpec as P

HEAD_DIM = 128
TILE = 256
SCALE = 1.0 / math.sqrt(HEAD_DIM)
F32 = jnp.float32
BF16 = jnp.bfloat16
SEQ = ("ylo", "z", "core")
HEAD = ("x", "yhi")
NT = (((1,), (1,)), ((), ()))
TN = (((0,), (0,)), ((), ()))


def tile_of(ref, u, before, after, count):
    if u < 0:
        return before[...]
    if u >= count:
        return after[...]
    return ref[u * TILE : (u + 1) * TILE, :]


def forward_kernel(bias, q, k, v, kb, vb, ka, va, attn, pt):
    count = q.shape[0] // TILE
    for t in range(count):
        rows = slice(t * TILE, (t + 1) * TILE)
        q_t = q[rows, :]
        parts = []
        for j in range(3):
            u = t + j - 1
            s = lax.dot_general(
                tile_of(k, u, kb, ka, count), q_t, NT, preferred_element_type=F32
            )
            if u < 0:
                s = s + bias[0]
            if u >= count:
                s = s + bias[1]
            parts.append(s)
        top = jnp.maximum(jnp.maximum(parts[0], parts[1]), parts[2])
        top = jnp.max(top, axis=0, keepdims=True)
        parts = [jnp.exp((s - top) * SCALE) for s in parts]
        total = jnp.sum(parts[0] + parts[1] + parts[2], axis=0, keepdims=True)
        inverse = 1.0 / total
        out = jnp.zeros((TILE, HEAD_DIM), F32)
        for j in range(3):
            w = (parts[j] * inverse).astype(BF16)
            pt[0, t, j * TILE : (j + 1) * TILE, :] = w
            out += lax.dot_general(
                w, tile_of(v, t + j - 1, vb, va, count), TN, preferred_element_type=F32
            )
        attn[rows, :] = out.astype(BF16)


def backward_kernel(q, k, v, kb, vb, ka, va, pt, keep, recv, first, dx, hb, ha):
    count = q.shape[0] // TILE
    h = pl.program_id(0)
    width = 2 * HEAD_DIM
    dk = [jnp.zeros((TILE, HEAD_DIM), F32) for _ in range(count + 2)]
    dv = [jnp.zeros((TILE, HEAD_DIM), F32) for _ in range(count + 2)]
    col = [pl.ds(pl.multiple_of(n * width + h * HEAD_DIM, HEAD_DIM), HEAD_DIM) for n in range(3)]
    for t in range(count):
        rows = slice(t * TILE, (t + 1) * TILE)
        q_t = q[rows, :]
        do = (keep[rows, :] + recv[rows, :].astype(F32)).astype(BF16)
        dps, ws = [], []
        delta = jnp.zeros((1, TILE), F32)
        for j in range(3):
            dp = lax.dot_general(
                tile_of(v, t + j - 1, vb, va, count), do, NT, preferred_element_type=F32
            )
            w = pt[0, t, j * TILE : (j + 1) * TILE, :]
            delta += jnp.sum(w.astype(F32) * dp, axis=0, keepdims=True)
            dps.append(dp)
            ws.append(w)
        dq = jnp.zeros((TILE, HEAD_DIM), F32)
        for j in range(3):
            ds = (ws[j].astype(F32) * (dps[j] - delta)).astype(BF16)
            dv[t + j] += jnp.dot(ws[j], do, preferred_element_type=F32)
            dk[t + j] += jnp.dot(ds, q_t, preferred_element_type=F32)
            dq += lax.dot_general(
                ds, tile_of(k, t + j - 1, kb, ka, count), TN, preferred_element_type=F32
            )
        dx[rows, col[0]] = (dq * SCALE).astype(BF16)
    for u in range(count + 2):
        a = (dk[u] * SCALE).astype(BF16)
        b = dv[u].astype(BF16)
        if u == 0:
            hb[:, col[0]] = a
            hb[:, col[1]] = b
        elif u == count + 1:
            ha[:, col[0]] = a
            ha[:, col[1]] = b
        else:
            rows = slice((u - 1) * TILE, u * TILE)
            dx[rows, col[1]] = a
            dx[rows, col[2]] = b


def column(rows, offset):
    return pl.BlockSpec((rows, HEAD_DIM), lambda h: (0, offset + h))


def tile_specs(rows):
    return [
        column(rows, 0),
        column(rows, 2),
        column(rows, 4),
        column(TILE, 0),
        column(TILE, 2),
        column(TILE, 0),
        column(TILE, 2),
    ]


def attention_forward(bias, x, before, after):
    rows = x.shape[0]
    count = rows // TILE
    return pl.pallas_call(
        forward_kernel,
        grid=(2,),
        in_specs=[pl.BlockSpec(memory_space=pltpu.SMEM)] + tile_specs(rows),
        out_specs=[
            column(rows, 0),
            pl.BlockSpec((1, count, 3 * TILE, TILE), lambda h: (h, 0, 0, 0)),
        ],
        out_shape=[
            jax.ShapeDtypeStruct((rows, 2 * HEAD_DIM), BF16),
            pltpu.HBM((2, count, 3 * TILE, TILE), BF16),
        ],
        compiler_params=pltpu.CompilerParams(vmem_limit_bytes=40 * 1024 * 1024),
        cost_estimate=pl.CostEstimate(
            flops=2 * 2 * 2 * rows * 3 * TILE * HEAD_DIM,
            bytes_accessed=6 * 1024 * 1024,
            transcendentals=2 * rows * 3 * TILE,
        ),
        name="forward",
    )(bias, x, x, x, before, before, after, after)


def attention_backward(x, before, after, pt, keep, recv, first):
    rows = x.shape[0]
    count = rows // TILE
    return pl.pallas_call(
        backward_kernel,
        grid=(2,),
        in_specs=tile_specs(rows)
        + [
            pl.BlockSpec((1, count, 3 * TILE, TILE), lambda h: (h, 0, 0, 0)),
            column(rows, 0),
            column(rows, 0),
            pl.BlockSpec(memory_space=pl.ANY),
        ],
        out_specs=[
            pl.BlockSpec((rows, 6 * HEAD_DIM), lambda h: (0, 0)),
            pl.BlockSpec((TILE, 4 * HEAD_DIM), lambda h: (0, 0)),
            pl.BlockSpec((TILE, 4 * HEAD_DIM), lambda h: (0, 0)),
        ],
        out_shape=[
            pltpu.HBM((rows, 6 * HEAD_DIM), BF16),
            jax.ShapeDtypeStruct((TILE, 4 * HEAD_DIM), BF16),
            jax.ShapeDtypeStruct((TILE, 4 * HEAD_DIM), BF16),
        ],
        compiler_params=pltpu.CompilerParams(vmem_limit_bytes=40 * 1024 * 1024),
        cost_estimate=pl.CostEstimate(
            flops=2 * 4 * 2 * rows * 3 * TILE * HEAD_DIM,
            bytes_accessed=9 * 1024 * 1024,
            transcendentals=0,
        ),
        name="backward",
    )(x, x, x, before, before, after, after, pt, keep, recv, first)


def pack_kernel(q, k, v, out):
    width = 2 * HEAD_DIM
    for g in range(out.shape[0]):
        for n, ref in enumerate((q, k, v)):
            out[g, :, n * width : (n + 1) * width] = ref[:, g * width : (g + 1) * width]


def pack(q, k, v):
    rows, full = q.shape
    width = 2 * HEAD_DIM
    groups = full // width
    part = pl.BlockSpec((rows, 2 * width), lambda i: (0, i))
    return pl.pallas_call(
        pack_kernel,
        grid=(groups // 2,),
        in_specs=[part] * 3,
        out_specs=pl.BlockSpec((2, rows, 3 * width), lambda i: (i, 0, 0)),
        out_shape=jax.ShapeDtypeStruct((groups, rows, 3 * width), BF16),
        cost_estimate=pl.CostEstimate(flops=0, bytes_accessed=3 << 20, transcendentals=0),
        name="pack",
    )(q, k, v)


def dout_kernel(where, og, own, other, first, keep, send, weight):
    size, rows, _ = own.shape
    width = keep.shape[1]

    @pl.when(pl.program_id(0) == 0)
    def _():
        near = pl.ds(pl.multiple_of((1 - where[1]) * width, width), width)
        far = pl.ds(pl.multiple_of(where[1] * width, width), width)
        for n in range(size):
            for ref, place in ((own, where[0]), (other, 1 - where[0])):
                to = pl.ds(pl.multiple_of((2 * n + place) * rows, rows), rows)
                weight[to, near] = ref[n, :, :width]
                weight[to, far] = ref[n, :, width:]

    out = jnp.dot(og[...], weight[...], preferred_element_type=F32)
    keep[...] = out[:, :width]
    send[...] = out[:, width:].astype(BF16)


def dout_parts(where, og, own, other, first):
    rows, half = og.shape
    size, depth, both = own.shape
    width = both // 2
    block = rows // 4
    whole = pl.BlockSpec((size, depth, both), lambda i, w: (0, 0, 0))
    return pl.pallas_call(
        dout_kernel,
        grid_spec=pltpu.PrefetchScalarGridSpec(
            num_scalar_prefetch=1,
            grid=(4,),
            in_specs=[pl.BlockSpec((block, half), lambda i, w: (i, 0)), whole, whole]
            + [pl.BlockSpec(memory_space=pl.ANY)],
            out_specs=[pl.BlockSpec((block, width), lambda i, w: (i, 0))] * 2,
            scratch_shapes=[pltpu.VMEM((half, both), BF16)],
        ),
        out_shape=[
            pltpu.HBM((rows, width), F32),
            jax.ShapeDtypeStruct((rows, width), BF16),
        ],
        compiler_params=pltpu.CompilerParams(vmem_limit_bytes=40 * 1024 * 1024),
        cost_estimate=pl.CostEstimate(
            flops=2 * rows * half * both, bytes_accessed=7 << 20, transcendentals=0
        ),
        name="dout",
    )(where, og, own, other, first)


def projection_kernel(where, og, attn, attn_other, first, mine, rest, other, total):
    depth = mine.shape[1]
    width = attn.shape[1]
    near = pl.ds(pl.multiple_of((1 - where[1]) * width, width), width)
    far = pl.ds(pl.multiple_of(where[1] * width, width), width)
    total[:, near] = lax.dot_general(og[...], attn[...], TN, preferred_element_type=F32)
    total[:, far] = lax.dot_general(og[...], attn_other[...], TN, preferred_element_type=F32)
    own = where[0] * depth
    for n in range(mine.shape[0]):
        first = pl.ds(pl.multiple_of(2 * n * depth + own, depth), depth)
        second = pl.ds(pl.multiple_of((2 * n + 1) * depth - own, depth), depth)
        mine[n] = total[first, :width]
        rest[n] = total[first, width:].astype(BF16)
        other[n] = total[second, :].astype(BF16)


def projection_grad(where, og, attn, attn_other, first, size):
    rows, half = og.shape
    width = attn.shape[1]
    depth = half // (2 * size)
    steps = 4
    whole = pl.BlockSpec((rows, width), lambda i, w: (0, 0))
    part = pl.BlockSpec((size // steps, depth, 2 * width), lambda i, w: (i, 0, 0))
    narrow = pl.BlockSpec((size // steps, depth, width), lambda i, w: (i, 0, 0))
    return pl.pallas_call(
        projection_kernel,
        grid_spec=pltpu.PrefetchScalarGridSpec(
            num_scalar_prefetch=1,
            grid=(steps,),
            in_specs=[pl.BlockSpec((rows, half // steps), lambda i, w: (0, i)), whole, whole]
            + [pl.BlockSpec(memory_space=pl.ANY)],
            out_specs=[narrow, narrow, part],
            scratch_shapes=[pltpu.VMEM((half // steps, 2 * width), F32)],
        ),
        out_shape=[
            jax.ShapeDtypeStruct((size, depth, width), F32),
            jax.ShapeDtypeStruct((size, depth, width), BF16),
            jax.ShapeDtypeStruct((size, depth, 2 * width), BF16),
        ],
        compiler_params=pltpu.CompilerParams(vmem_limit_bytes=60 * 1024 * 1024),
        cost_estimate=pl.CostEstimate(
            flops=2 * rows * half * 2 * width, bytes_accessed=7 << 20, transcendentals=0
        ),
        name="projection",
    )(where, og, attn, attn_other, first)


def edges_kernel(dx, low, high, out):
    width = 2 * HEAD_DIM
    out[:, :width] = dx[:, :width]
    added = jnp.where(pl.program_id(0) == 0, low[...].astype(F32), high[...].astype(F32))
    out[:, width:] = (dx[:, width:].astype(F32) + added).astype(BF16)


def add_edges(dx, low, high):
    rows, full = dx.shape
    last = rows // TILE - 1
    part = pl.BlockSpec((TILE, full), lambda i: (i * last, 0))
    edge = pl.BlockSpec(low.shape, lambda i: (0, 0))
    return pl.pallas_call(
        edges_kernel,
        grid=(2,),
        in_specs=[part, edge, edge],
        out_specs=part,
        out_shape=jax.ShapeDtypeStruct(dx.shape, BF16),
        input_output_aliases={0: 0},
        cost_estimate=pl.CostEstimate(flops=0, bytes_accessed=2 << 20, transcendentals=0),
        name="edges",
    )(dx, low, high)


def tie_kernel(*refs):
    pass


def tie(array, *first):
    spec = pl.BlockSpec(memory_space=pl.ANY)
    return pl.pallas_call(
        tie_kernel,
        in_specs=[spec] * (1 + len(first)),
        out_specs=spec,
        out_shape=jax.ShapeDtypeStruct(array.shape, array.dtype),
        input_output_aliases={0: 0},
        cost_estimate=pl.CostEstimate(flops=0, bytes_accessed=0, transcendentals=0),
        name="tie",
    )(array, *first)


def swapped(array, axis):
    return lax.ppermute(array, axis, [(0, 1), (1, 0)])


Y = ("ylo", "yhi")
FAR = [(2, 0), (1, 3), (0, 1), (3, 2)]
NEAR = [(1, 2), (2, 1)]


def from_owners(block, same):
    far = lax.ppermute(block, Y, [(j, i) for i, j in FAR])
    near = lax.ppermute(block, Y, NEAR)
    return jnp.where(same, block, near), far


def to_neighbours(down_part, up_part):
    count = lax.axis_size(SEQ)
    up = [(i, i + 1) for i in range(count - 1)]
    down = [(j, i) for i, j in up]
    return lax.ppermute(up_part, SEQ, up), lax.ppermute(down_part, SEQ, down)


def reduced_along_z(array):
    size = lax.axis_size("z")
    place = lax.axis_index("z")
    step = 1
    while step < size // 2:
        halves = array.reshape((-1, 2) + array.shape[1:])
        bit = (place // step) % 2
        own = lax.dynamic_index_in_dim(halves, bit, 1, keepdims=False)
        send = lax.dynamic_index_in_dim(halves, 1 - bit, 1, keepdims=False)
        other = lax.ppermute(send.astype(BF16), "z", [(i, i ^ step) for i in range(size)])
        array = own + other.astype(F32)
        step *= 2
    bit = place // step
    own = lax.dynamic_index_in_dim(array, bit, 0, keepdims=False)
    send = lax.dynamic_index_in_dim(array, 1 - bit, 0, keepdims=False)
    axes = ("ylo", "z", "yhi")

    def pairs(flip):
        at = lambda a, z, b: (a * size + z) * 2 + b
        return [
            (at(a, z, b), at(b, z ^ flip, a)) for a in range(2) for z in range(size) for b in range(2)
        ]

    near = lax.ppermute(own, axes, pairs(0))
    far = lax.ppermute(send, axes, pairs(step))
    return near, far


def per_device(queries, keys, values, out_grad, out_weight):
    ylo, core, yhi = (lax.axis_index(a) for a in ("ylo", "core", "yhi"))
    z_count = lax.axis_size("z")
    place = lax.axis_index(SEQ)
    groups = lax.axis_size(HEAD)
    width = 2 * HEAD_DIM
    rows_own = queries.shape[0]
    half = out_grad.shape[1] // 2
    same = ylo == yhi
    where = jnp.stack([core, same]).astype(jnp.int32)

    owned = lax.all_gather(out_weight, "z", axis=0)
    weight = jnp.concatenate(from_owners(owned, same), axis=2)

    og_own = lax.dynamic_slice_in_dim(out_grad, yhi * half, half, 1)
    og_send = lax.dynamic_slice_in_dim(out_grad, (1 - yhi) * half, half, 1)
    og_other = swapped(og_send, "yhi")
    og = jnp.concatenate(
        [jnp.where(yhi == 0, og_own, og_other), jnp.where(yhi == 0, og_other, og_own)], axis=0
    )
    og = jnp.broadcast_to(og[None], (lax.axis_size("x"),) + og.shape)

    x = pack(queries, keys, values)
    x = lax.all_to_all(x, HEAD, 0, 0, tiled=True).reshape(-1, 3 * width)
    rows = x.shape[0]
    before, after = to_neighbours(x[:TILE, width:], x[rows - TILE :, width:])

    og = lax.all_to_all(tie(og, x, owned), "x", 0, 0, tiled=True).reshape(rows, half)

    edge = jnp.stack([place == 0, place == lax.axis_size(SEQ) - 1])
    bias = jnp.where(edge, -1e30, 0.0).astype(F32)
    attn, pt = attention_forward(bias, x, before, after)
    attn_other = swapped(attn, "yhi")
    weight = tie(weight, attn)
    weight_other = swapped(weight, "core")

    near, far, other = projection_grad(where, og, attn, attn_other, weight, z_count)
    from_core = swapped(other, "core").astype(F32)
    far = (far.astype(F32) + from_core[:, :, width:]).astype(BF16)
    near = near + from_core[:, :, :width]
    parts = reduced_along_z(near + swapped(far, "ylo").astype(F32))

    dout_keep, dout_send = dout_parts(where, og, weight, weight_other, other)
    dout_recv = swapped(dout_send, "yhi")

    dx, dx_before, dx_after = attention_backward(
        x, before, after, pt, dout_keep, dout_recv, far
    )
    from_left, from_right = to_neighbours(dx_before, dx_after)
    dx = add_edges(dx, from_left, from_right)
    dx = lax.all_to_all(dx.reshape(groups, rows_own, 3 * width), HEAD, 0, 0, tiled=True)
    grads = [
        dx[:, :, n * width : (n + 1) * width].transpose(1, 0, 2).reshape(rows_own, -1)
        for n in range(3)
    ]
    return (*grads, tie(parts[0], grads[0]) + parts[1])


def solution(mesh):
    sizes = (2, mesh.shape["seq"] // 4, 2, mesh.shape["head"] // 2, 2)
    fine = Mesh(mesh.devices.reshape(sizes), ("ylo", "z", "core", "x", "yhi"))
    tokens = P((*SEQ, *HEAD), None)
    weight = P(SEQ, HEAD)
    return jax.shard_map(
        per_device,
        mesh=fine,
        in_specs=(tokens, tokens, tokens, tokens, weight),
        out_specs=(tokens, tokens, tokens, weight),
        check_vma=False,
    )
```
